32 devices in a mesh: row: 4 (over y, x), col: 8 (over z, core).
Axes of the slice: x: 2, y: 2, z: 4, core: 2. Of those that a mesh axis runs over, the one named last changes fastest.
Arguments:
- features: bfloat16 [8, 4096, 128], P('col', 'row'), may hold values from 0.099609375 to 3
- relu_mask: int32 [8, 4096, 128], P('col', 'row'), may hold values 0 or 1
- tiles: bfloat16 [4, 8, 184, 256, 256], P('row', 'col'), may hold values from -0.25 to 0.25
- tile_rows: int32 [4, 8, 184], P('row', 'col'), may hold values from 0 to 31, as said below
- tile_cols: int32 [4, 8, 184], P('row', 'col'), may hold values from 0 to 15
- tile_count: int32 [4, 8], P('row', 'col'), may hold values from 23 to 184, as said below
- weight: bfloat16 [128, 128], replicated, may hold values from -0.5 to 0.5
- cotangent: bfloat16 [4, 8192, 128], P('row', 'col'), may hold values from -6 to 6
Outputs:
- out_pre: bfloat16 [4, 8192, 128], P('row', 'col')
- weight_grad: float32 [128, 128], replicated
- input_grad: bfloat16 [8, 4096, 128], P('col', 'row')
The draws below stay inside these ranges and needn't reach their ends.
Inputs may be any that keep to these rules, and one draw needn't show every extreme that they name: `tile_rows`: within one panel pair the live and dead slots name distinct (block row, block column) pairs. `tile_count`: counts differ widely between panel pairs.
All inputs are finite; a program needn't handle non-finite values. No bound on the sum of `relu_mask` on one device may be relied on, other than what follows from the above.
Results may differ from the reference program's by a relative error of at most 0.022.
Values may be sent and summed in bfloat16 or wider, within the bound.
No kernel may reach another device: no remote copies, remote signals or barrier semaphores. Data moves between devices by JAX's collectives and lax.ppermute only.
A program may use at most 192 MiB of HBM per device.

```python
import math
import jax
import jax.numpy as jnp
from jax import lax

F = 128
TILE = 256
NODES_DEV = 1024
CAP = 184
ROW_PANEL = 8192
COL_PANEL = 4096
N_ROW = 4
N_COL = 8
DEVICES = 32


def tile_layout(key):
    base_key = jax.random.fold_in(key, 11)
    key_perm, key_level, key_full = jax.random.split(base_key, 3)
    row_blocks = NODES_DEV * N_COL // TILE
    col_blocks = NODES_DEV * N_ROW // TILE
    device_keys = jax.random.split(key_perm, N_ROW * N_COL)
    picks = jax.vmap(lambda one_key: jax.random.permutation(one_key, row_blocks * col_blocks)[:CAP])(device_keys)
    picks = picks.reshape(N_ROW, N_COL, CAP).astype(jnp.int32)
    levels = jax.random.randint(key_level, (N_ROW, N_COL), 0, 4).astype(jnp.int32)
    counts = jnp.int32(CAP) // jnp.left_shift(jnp.int32(1), levels)
    busiest = jax.random.randint(key_full, (), 0, N_ROW * N_COL).astype(jnp.int32)
    flat_ids = jnp.arange(N_ROW * N_COL, dtype=jnp.int32).reshape(N_ROW, N_COL)
    counts = jnp.where(flat_ids == busiest, jnp.int32(CAP), counts).astype(jnp.int32)
    return (picks // col_blocks, picks % col_blocks, counts)


def draw_tile_rows(key, part):
    return tile_layout(key)[0]


def draw_tile_cols(key, part):
    return tile_layout(key)[1]


def draw_tile_count(key, part):
    return tile_layout(key)[2]


def place_ends(result, key, low, largest):
    spot = [jax.random.randint(jax.random.fold_in(key, axis), (), 0, length) for axis, length in enumerate(result.shape)]
    main_axis = result.shape.index(max(result.shape))
    neighbour = spot[:main_axis] + [(spot[main_axis] + 1) % result.shape[main_axis]] + spot[main_axis + 1:]
    return result.at[tuple(spot)].set(low).at[tuple(neighbour)].set(largest)


def level_of(stream_key, shape, shards, low, largest):
    loudness = 1.0
    for position, shards_of in shards:
        heights = jax.random.uniform(jax.random.fold_in(jax.random.fold_in(stream_key, 6), position), (shards_of,), jnp.float32, low / len(shards), largest / len(shards))
        loudness = loudness * jnp.repeat(jnp.exp(heights), shape[position] // shards_of).reshape((-1,) + (1,) * (len(shape) - 1 - position))
    return loudness


def normal_values(stream_key, dims, spread, reach, shards=(), kind=jnp.bfloat16):
    array = spread * jax.random.normal(stream_key, dims, jnp.float32)
    if shards:
        array = array * level_of(stream_key, dims, shards, -0.22, 0.18)
    return jnp.clip(array, -reach, reach).astype(kind)


def setup_inputs(seed: int = 0) -> dict:
    key_list = jax.random.split(jax.random.key(seed), 9)
    features = jnp.clip(jnp.exp(math.log(3.0) - 3.4051113 * jax.random.uniform(key_list[0], (N_COL, COL_PANEL, F), jnp.float32) ** level_of(key_list[0], (N_COL, COL_PANEL, F), ((0, 8), (1, 4)), -0.2, 0.2)), 0.099609375, 3.0).astype(jnp.bfloat16)
    relu_mask = place_ends((jax.random.randint(key_list[1], (N_COL, COL_PANEL, F), 0, 2) < 1).astype(jnp.int32), jax.random.fold_in(key_list[1], 1), 0, 1)
    tiles = normal_values(key_list[2], (N_ROW, N_COL, CAP, TILE, TILE), ((CAP * TILE * TILE // (3 * NODES_DEV)) ** -0.5), 0.25, ((0, 4), (1, 8)))
    tile_rows = draw_tile_rows(jax.random.fold_in(key_list[8], 71), 0)
    tile_cols = draw_tile_cols(jax.random.fold_in(key_list[8], 71), 0)
    tile_count = draw_tile_count(jax.random.fold_in(key_list[8], 71), 0)
    weight = normal_values(key_list[6], (F, F), F ** -0.5, 0.5)
    cotangent = normal_values(key_list[7], (N_ROW, ROW_PANEL, F), 1.0, 6.0, ((0, 4), (1, 8)))
    return {"features": features, "relu_mask": relu_mask, "tiles": tiles, "tile_rows": tile_rows, "tile_cols": tile_cols, "tile_count": tile_count, "weight": weight, "cotangent": cotangent}


def forward_part(tile_vals, row_ids, col_ids, live_count, feat_panel):
    blocks = feat_panel.reshape(-1, TILE, F)[col_ids].astype(jnp.float32)
    products = jnp.einsum('sij,sjf->sif', tile_vals.astype(jnp.float32), blocks)
    live_slots = jnp.arange(CAP, dtype=jnp.int32) < live_count
    products = jnp.where(live_slots[:, None, None], products, 0.0)
    total = jax.ops.segment_sum(products, row_ids, num_segments=NODES_DEV * N_COL // TILE)
    return total.reshape(-1, F)

def backward_part(tile_vals, row_ids, col_ids, live_count, grad_rows):
    blocks = grad_rows.reshape(-1, TILE, F)[row_ids].astype(jnp.float32)
    products = jnp.einsum('sij,sif->sjf', tile_vals.astype(jnp.float32), blocks)
    live_slots = jnp.arange(CAP, dtype=jnp.int32) < live_count
    products = jnp.where(live_slots[:, None, None], products, 0.0)
    total = jax.ops.segment_sum(products, col_ids, num_segments=NODES_DEV * N_ROW // TILE)
    return total.reshape(-1, F)

def reference(features, relu_mask, tiles, tile_rows, tile_cols, tile_count, weight, cotangent):
    hidden = features * relu_mask.astype(jnp.bfloat16)

    def row_panel(row_index):

        def panel_step(running, inputs):
            tile_vals, row_ids, col_ids, live_count, feat_panel = inputs
            partial_value = forward_part(tile_vals, row_ids, col_ids, live_count, feat_panel)
            rounded = lax.optimization_barrier(partial_value.astype(jnp.bfloat16))
            return (running + rounded.astype(jnp.float32), None)
        running, unused = lax.scan(panel_step, jnp.zeros((NODES_DEV * N_COL, F), jnp.float32), (tiles[row_index], tile_rows[row_index], tile_cols[row_index], tile_count[row_index], hidden))
        return running.astype(jnp.bfloat16)
    aggregate = lax.map(row_panel, jnp.arange(N_ROW, dtype=jnp.int32))
    flat_agg = aggregate.reshape(-1, F)
    flat_cot = cotangent.reshape(-1, F)
    out_pre = jnp.dot(flat_agg, weight, preferred_element_type=jnp.float32).astype(jnp.bfloat16)
    out_pre = out_pre.reshape(N_ROW, NODES_DEV * N_COL, F)
    grad_scale = 1.0 / jnp.sqrt(jnp.float32(NODES_DEV * DEVICES))
    weight_grad = jnp.dot(flat_agg.T, flat_cot, preferred_element_type=jnp.float32) * grad_scale
    grad_agg = jnp.dot(flat_cot, weight.T, preferred_element_type=jnp.float32).astype(jnp.bfloat16)
    grad_agg = grad_agg.reshape(N_ROW, NODES_DEV * N_COL, F)

    def col_panel(col_index):

        def panel_step(running, inputs):
            tile_vals, row_ids, col_ids, live_count, grad_rows = inputs
            partial_value = backward_part(tile_vals, row_ids, col_ids, live_count, grad_rows)
            rounded = lax.optimization_barrier(partial_value.astype(jnp.bfloat16))
            return (running + rounded.astype(jnp.float32), None)
        running, unused = lax.scan(panel_step, jnp.zeros((NODES_DEV * N_ROW, F), jnp.float32), (tiles[:, col_index], tile_rows[:, col_index], tile_cols[:, col_index], tile_count[:, col_index], grad_agg))
        return running
    back_terms = lax.map(col_panel, jnp.arange(N_COL, dtype=jnp.int32))
    input_grad = (back_terms * relu_mask.astype(jnp.float32)).astype(jnp.bfloat16)
    return (out_pre, weight_grad, input_grad)
```

```python
import functools
import math

import jax
import jax.numpy as jnp
from jax import lax
from jax.experimental import pallas as pl
from jax.experimental.pallas import tpu as pltpu
from jax.sharding import PartitionSpec as P

CORES = 2
VMEM_LIMIT = 50 * 2**20
F32 = jnp.float32
BF16 = jnp.bfloat16
ANY = pl.BlockSpec(memory_space=pl.ANY)
SMEM = pl.BlockSpec(memory_space=pltpu.SMEM)
VMEM = pl.BlockSpec(memory_space=pltpu.VMEM)
PARAMS = pltpu.CompilerParams(vmem_limit_bytes=VMEM_LIMIT)


def swap(value, axis, step):
    size = lax.axis_size(axis)
    return lax.ppermute(value, axis, [(i, i ^ step) for i in range(size)])


def chunk_of(slots):
    return math.gcd(slots, 8)


def tile_copies(tiles, buf, sems):
    chunk = chunk_of(buf.shape[0])

    def copy(i):
        span = pl.ds(i * chunk, chunk)
        return pltpu.make_async_copy(tiles.at[0, 0, span], buf.at[span], sems.at[i])

    return copy


def forward_kernel(n_shards, count_ref, rows_ref, cols_ref, tiles, *refs):
    shards, (keep, send) = refs[:n_shards], refs[n_shards : n_shards + 2]
    buf, panel, acc, tile_sems, panel_sems = refs[n_shards + 2 :]
    slots, tile = buf.shape[:2]
    own = shards[0].shape[0]
    chunk = chunk_of(slots)
    dump = acc.shape[0] - 1
    live = count_ref[0, 0]
    chunks = pl.cdiv(live, chunk)
    row, col = lax.axis_index("row"), lax.axis_index("col")
    line, core = col // CORES, col % CORES
    copy = tile_copies(tiles, buf, tile_sems)

    def panel_copy(k):
        place = pl.multiple_of((row ^ k) * own, own)
        return pltpu.make_async_copy(shards[k], panel.at[pl.ds(place, own)], panel_sems.at[k])

    for k in range(n_shards):
        panel_copy(k).start()

    @pl.loop(0, chunks)
    def _(i):
        copy(i).start()

    acc[...] = jnp.zeros_like(acc)
    for k in range(n_shards):
        panel_copy(k).wait()

    @pl.loop(0, chunks)
    def _(i):
        copy(i).wait()
        for j in range(chunk):
            s = i * chunk + j
            c = cols_ref[0, 0, s]
            r = jnp.where(s < live, rows_ref[0, 0, s], dump)
            source = panel[pl.ds(pl.multiple_of(c * tile, tile), tile), :]
            acc[r] += jnp.dot(buf[s], source, preferred_element_type=F32)

    per = own // tile
    for k in range(keep.shape[0] // own):
        base = (line ^ k) * CORES
        for b in range(per):
            span = pl.ds(k * own + b * tile, tile)
            keep[span, :] = acc[(base + core) * per + b].astype(BF16)
            send[span, :] = acc[(base + 1 - core) * per + b].astype(BF16)


def backward_kernel(n_rows, n_lines, count_ref, rows_ref, cols_ref, tiles, scale, *refs):
    n_cots = n_lines * CORES
    hids, cots, refs = refs[:n_rows], refs[n_rows : n_rows + n_cots], refs[n_rows + n_cots :]
    outs, weight_term, refs = refs[:n_rows], refs[n_rows], refs[n_rows + 1 :]
    buf, panel, turned, hidden, acc, tile_sems, panel_sems = refs
    slots, tile = buf.shape[:2]
    own = hids[0].shape[0]
    per = own // tile
    chunk = chunk_of(slots)
    dump = acc.shape[0] - 1
    live = count_ref[0, 0]
    chunks = pl.cdiv(live, chunk)
    row, col = lax.axis_index("row"), lax.axis_index("col")
    line, core = col // CORES, col % CORES
    copy = tile_copies(tiles, buf, tile_sems)

    def cot_copy(k):
        place = ((line ^ (k // CORES)) * CORES + (core ^ (k % CORES))) * own
        span = pl.ds(pl.multiple_of(place, own), own)
        return pltpu.make_async_copy(cots[k], panel.at[span], panel_sems.at[k])

    def hid_copy(k):
        span = pl.ds(pl.multiple_of((row ^ k) * own, own), own)
        return pltpu.make_async_copy(hids[k], hidden.at[span], panel_sems.at[n_cots + k])

    for k in range(n_cots):
        cot_copy(k).start()

    @pl.loop(0, chunks)
    def _(i):
        copy(i).start()

    for k in range(n_rows):
        hid_copy(k).start()
    acc[...] = jnp.zeros_like(acc)
    for k in range(n_cots):
        cot_copy(k).wait()
    for b in range(turned.shape[0]):
        turned[b] = panel[b * tile : (b + 1) * tile, :].T

    @pl.loop(0, chunks)
    def _(i):
        copy(i).wait()
        for j in range(chunk):
            s = i * chunk + j
            r = rows_ref[0, 0, s]
            c = jnp.where(s < live, cols_ref[0, 0, s], dump)
            acc[c] += jnp.dot(turned[r], buf[s], preferred_element_type=F32)

    for k in range(n_rows):
        hid_copy(k).wait()
    total = jnp.zeros(weight_term.shape, F32)
    for b in range(acc.shape[0] - 1):
        total += jnp.dot(
            acc[b].astype(BF16), hidden[b * tile : (b + 1) * tile, :], preferred_element_type=F32
        )
    weight_term[...] = total.T * scale[0]
    for k in range(n_rows):
        for b in range(per):
            outs[k][b * tile : (b + 1) * tile, :] = acc[(row ^ k) * per + b].T.astype(BF16)


def pair_kernel(keep, got, *outs):
    own = outs[0].shape[0]
    for k, out in enumerate(outs):
        span = pl.ds(k * own, own)
        out[...] = (keep[span, :].astype(F32) + got[span, :].astype(F32)).astype(BF16)


def summed(parts):
    total = parts[0][...].astype(F32)
    for part in parts[1:]:
        total += part[...].astype(F32)
    return total.astype(BF16)


def out_kernel(weight, *refs):
    refs[-1][0] = jnp.dot(summed(refs[:-1]), weight[...], preferred_element_type=F32).astype(BF16)


def grad_kernel(weight, mask, *refs):
    turned = lax.dot_general(
        summed(refs[:-1]), weight[...], (((1,), (1,)), ((), ())), preferred_element_type=F32
    )
    refs[-1][0] = (turned * mask[0].astype(F32)).astype(BF16)


def body(features, relu_mask, tiles, tile_rows, tile_cols, tile_count, weight, cotangent):
    slots, tile = tiles.shape[2:4]
    own, width = features.shape[1:]
    n_rows, n_cols = lax.axis_size("row"), lax.axis_size("col")
    n_lines = n_cols // CORES
    row_blocks, col_blocks = own * n_cols // tile, own * n_rows // tile
    ids = (tile_count, tile_rows, tile_cols, tiles)
    block = jax.ShapeDtypeStruct((own, width), BF16)

    cot = cotangent[0]
    cots = [cot] + [swap(cot, "col", CORES * k) for k in range(1, n_lines)]
    cots = [part for mine in cots for part in (mine, swap(mine, "col", 1))]
    hidden = features[0] * relu_mask[0].astype(BF16)
    hids = [hidden] + [swap(hidden, "row", k) for k in range(1, n_rows)]

    half = jax.ShapeDtypeStruct((n_lines * own, width), BF16)
    keep, send = pl.pallas_call(
        functools.partial(forward_kernel, n_rows),
        out_shape=(half, half),
        in_specs=[SMEM] * 3 + [ANY] * (1 + n_rows),
        out_specs=(VMEM, VMEM),
        scratch_shapes=[
            pltpu.VMEM((slots, tile, tile), BF16),
            pltpu.VMEM((n_rows * own, width), BF16),
            pltpu.VMEM((row_blocks + 1, tile, width), F32),
            pltpu.SemaphoreType.DMA((slots // chunk_of(slots),)),
            pltpu.SemaphoreType.DMA((n_rows,)),
        ],
        compiler_params=PARAMS,
        name="forward_tiles",
    )(*ids, *hids)
    got = swap(send, "col", 1)
    pairs = pl.pallas_call(
        pair_kernel,
        out_shape=(block,) * n_lines,
        in_specs=[VMEM] * 2,
        out_specs=(VMEM,) * n_lines,
        name="pair_sum",
    )(keep, got)
    parts = [pairs[0]] + [swap(pairs[k], "col", CORES * k) for k in range(1, n_lines)]
    out_pre = pl.pallas_call(
        out_kernel,
        out_shape=jax.ShapeDtypeStruct((1, own, width), BF16),
        in_specs=[VMEM] * (1 + n_lines),
        out_specs=VMEM,
        name="out_pre",
    )(weight, *parts)

    scale = 1.0 / jnp.sqrt(jnp.full((1,), own * n_rows * n_cols, F32))
    *backs, weight_term = pl.pallas_call(
        functools.partial(backward_kernel, n_rows, n_lines),
        out_shape=(block,) * n_rows + (jax.ShapeDtypeStruct((width, width), F32),),
        in_specs=[SMEM] * 3 + [ANY] + [SMEM] + [ANY] * (n_rows + n_cols),
        out_specs=(VMEM,) * (n_rows + 1),
        scratch_shapes=[
            pltpu.VMEM((slots, tile, tile), BF16),
            pltpu.VMEM((n_cols * own, width), BF16),
            pltpu.VMEM((row_blocks, width, tile), BF16),
            pltpu.VMEM((n_rows * own, width), BF16),
            pltpu.VMEM((col_blocks + 1, width, tile), F32),
            pltpu.SemaphoreType.DMA((slots // chunk_of(slots),)),
            pltpu.SemaphoreType.DMA((n_cols + n_rows,)),
        ],
        compiler_params=PARAMS,
        name="backward_tiles",
    )(*ids, scale, *hids, *cots)
    backs = [backs[0]] + [swap(backs[k], "row", k) for k in range(1, n_rows)]
    input_grad = pl.pallas_call(
        grad_kernel,
        out_shape=jax.ShapeDtypeStruct((1, own, width), BF16),
        in_specs=[VMEM] * (2 + n_rows),
        out_specs=VMEM,
        name="input_grad",
    )(weight, relu_mask, *backs)

    for axis, size in (("col", n_cols), ("row", n_rows)):
        for bit in range(size.bit_length() - 1):
            weight_term = weight_term + swap(weight_term, axis, 1 << bit)
    return (out_pre, weight_term, input_grad)


def solution(mesh):
    placed = (
        P("col", "row", None),
        P("col", "row", None),
        P("row", "col", None, None, None),
        P("row", "col", None),
        P("row", "col", None),
        P("row", "col"),
        P(),
        P("row", "col", None),
    )
    return jax.shard_map(
        body,
        mesh=mesh,
        in_specs=placed,
        out_specs=(P("row", "col", None), P(), P("col", "row", None)),
        check_vma=False,
    )
```

```python
import functools
import math

import jax
import jax.numpy as jnp
from jax import lax
from jax.experimental import pallas as pl
from jax.experimental.pallas import tpu as pltpu
from jax.sharding import PartitionSpec as P

CORES = 2
MIB = 2**20
UNROLL = 23
WORK = 20
F32 = jnp.float32
BF16 = jnp.bfloat16
ANY = pl.BlockSpec(memory_space=pl.ANY)
SMEM = pl.BlockSpec(memory_space=pltpu.SMEM)
VMEM = pl.BlockSpec(memory_space=pltpu.VMEM)


def swap(value, axis, step):
    size = lax.axis_size(axis)
    return lax.ppermute(value, axis, [(i, i ^ step) for i in range(size)])


def room(size):
    return pltpu.CompilerParams(vmem_limit_bytes=size * MIB)


def cost(flops, moved):
    return pl.CostEstimate(flops=flops, bytes_accessed=moved, transcendentals=0)


def load_kernel(count_ref, tiles, held, sems):
    chunk = held.shape[0] // sems.shape[0]
    chunks = pl.cdiv(count_ref[0, 0], chunk)

    def copy(i):
        span = pl.ds(i * chunk, chunk)
        return pltpu.make_async_copy(tiles.at[0, 0, span], held.at[span], sems.at[i])

    @pl.loop(0, chunks)
    def _(i):
        copy(i).start()

    @pl.loop(0, chunks)
    def _(i):
        copy(i).wait()


def for_slots(live, slots, work):
    unroll = math.gcd(slots, UNROLL)

    @pl.loop(0, pl.cdiv(live, unroll))
    def _(i):
        for j in range(unroll):
            work(i * unroll + j)


def forward_kernel(n_shards, count_ref, rows_ref, cols_ref, tiles, *refs):
    shards, (keep, send) = refs[:n_shards], refs[n_shards : n_shards + 2]
    panel, acc = refs[n_shards + 2 :]
    slots, tile = tiles.shape[:2]
    own = shards[0].shape[0]
    dump = acc.shape[0] - 1
    live = count_ref[0, 0]
    row, col = lax.axis_index("row"), lax.axis_index("col")
    line, core = col // CORES, col % CORES

    acc[...] = jnp.zeros_like(acc)
    for k in range(n_shards):
        panel[pl.ds(pl.multiple_of((row ^ k) * own, own), own), :] = shards[k][...]

    def work(s):
        c = cols_ref[0, 0, s]
        r = jnp.where(s < live, rows_ref[0, 0, s], dump)
        source = panel[pl.ds(pl.multiple_of(c * tile, tile), tile), :]
        acc[r] += jnp.dot(tiles[s], source, preferred_element_type=F32)

    for_slots(live, slots, work)
    per = own // tile
    for k in range(keep.shape[0] // own):
        base = (line ^ k) * CORES
        for b in range(per):
            span = pl.ds(k * own + b * tile, tile)
            keep[span, :] = acc[(base + core) * per + b].astype(BF16)
            send[span, :] = acc[(base + 1 - core) * per + b].astype(BF16)


def backward_kernel(n_rows, n_lines, count_ref, rows_ref, cols_ref, tiles, scale, *refs):
    n_cots = n_lines * CORES
    hids, cots, refs = refs[:n_rows], refs[n_rows : n_rows + n_cots], refs[n_rows + n_cots :]
    outs, weight_term, refs = refs[:n_rows], refs[n_rows], refs[n_rows + 1 :]
    turned, acc = refs
    slots, tile = tiles.shape[:2]
    own = hids[0].shape[0]
    per = own // tile
    dump = acc.shape[0] - 1
    live = count_ref[0, 0]
    row, col = lax.axis_index("row"), lax.axis_index("col")
    line, core = col // CORES, col % CORES

    acc[...] = jnp.zeros_like(acc)
    for k in range(n_cots):
        place = ((line ^ (k // CORES)) * CORES + (core ^ (k % CORES))) * per
        for b in range(per):
            turned[place + b] = cots[k][b * tile : (b + 1) * tile, :].T

    def work(s):
        r = rows_ref[0, 0, s]
        c = jnp.where(s < live, cols_ref[0, 0, s], dump)
        acc[c] += jnp.dot(turned[r], tiles[s], preferred_element_type=F32)

    for_slots(live, slots, work)
    total = jnp.zeros(weight_term.shape, F32)
    for k in range(n_rows):
        for b in range(per):
            span = pl.ds(b * tile, tile)
            part = acc[(row ^ k) * per + b]
            total += jnp.dot(part.astype(BF16), hids[k][span, :], preferred_element_type=F32)
            outs[k][span, :] = part.T.astype(BF16)
    weight_term[...] = total.T * scale[0]


def pair_kernel(keep, got, *outs):
    own = outs[0].shape[0]
    for k, out in enumerate(outs):
        span = pl.ds(k * own, own)
        out[...] = (keep[span, :].astype(F32) + got[span, :].astype(F32)).astype(BF16)


def summed(parts):
    total = parts[0][...].astype(F32)
    for part in parts[1:]:
        total += part[...].astype(F32)
    return total.astype(BF16)


def out_kernel(weight, *refs):
    refs[-1][0] = jnp.dot(summed(refs[:-1]), weight[...], preferred_element_type=F32).astype(BF16)


def grad_kernel(weight, mask, *refs):
    turned = lax.dot_general(
        summed(refs[:-1]), weight[...], (((1,), (1,)), ((), ())), preferred_element_type=F32
    )
    refs[-1][0] = (turned * mask[0].astype(F32)).astype(BF16)


def body(features, relu_mask, tiles, tile_rows, tile_cols, tile_count, weight, cotangent):
    slots, tile = tiles.shape[2:4]
    own, width = features.shape[1:]
    n_rows, n_cols = lax.axis_size("row"), lax.axis_size("col")
    n_lines = n_cols // CORES
    row_blocks, col_blocks = own * n_cols // tile, own * n_rows // tile
    ids = (tile_count, tile_rows, tile_cols)
    block = jax.ShapeDtypeStruct((own, width), BF16)
    work = 2 * tiles.size * width

    cot = cotangent[0]
    cots = [cot] + [swap(cot, "col", CORES * k) for k in range(1, n_lines)]
    cots = [part for mine in cots for part in (mine, swap(mine, "col", 1))]
    hidden = features[0] * relu_mask[0].astype(BF16)
    hids = [hidden] + [swap(hidden, "row", k) for k in range(1, n_rows)]

    held = pl.pallas_call(
        load_kernel,
        out_shape=jax.ShapeDtypeStruct((slots, tile, tile), BF16),
        in_specs=[SMEM, ANY],
        out_specs=VMEM,
        scratch_shapes=[pltpu.SemaphoreType.DMA((slots // math.gcd(slots, 8),))],
        compiler_params=room(WORK),
        cost_estimate=cost(0, 2 * tiles.size),
        name="load_tiles",
    )(tile_count, tiles)

    half = jax.ShapeDtypeStruct((n_lines * own, width), BF16)
    keep, send = pl.pallas_call(
        functools.partial(forward_kernel, n_rows),
        out_shape=(half, half),
        in_specs=[SMEM] * 3 + [VMEM] * (1 + n_rows),
        out_specs=(VMEM, VMEM),
        scratch_shapes=[
            pltpu.VMEM((n_rows * own, width), BF16),
            pltpu.VMEM((row_blocks + 1, tile, width), F32),
        ],
        compiler_params=room(WORK),
        cost_estimate=cost(work, 2 * tiles.size),
        name="forward_tiles",
    )(*ids, held, *hids)
    got = swap(send, "col", 1)
    pairs = pl.pallas_call(
        pair_kernel,
        out_shape=(block,) * n_lines,
        in_specs=[VMEM] * 2,
        out_specs=(VMEM,) * n_lines,
        compiler_params=room(8),
        name="pair_sum",
    )(keep, got)
    parts = [pairs[0]] + [swap(pairs[k], "col", CORES * k) for k in range(1, n_lines)]
    out_pre = pl.pallas_call(
        out_kernel,
        out_shape=jax.ShapeDtypeStruct((1, own, width), BF16),
        in_specs=[VMEM] * (1 + n_lines),
        out_specs=VMEM,
        compiler_params=room(8),
        name="out_pre",
    )(weight, *parts)

    scale = 1.0 / jnp.sqrt(jnp.full((1,), own * n_rows * n_cols, F32))
    *backs, weight_term = pl.pallas_call(
        functools.partial(backward_kernel, n_rows, n_lines),
        out_shape=(block,) * n_rows + (jax.ShapeDtypeStruct((width, width), F32),),
        in_specs=[SMEM] * 3 + [VMEM] + [SMEM] + [VMEM] * (n_rows + n_cols),
        out_specs=(VMEM,) * (n_rows + 1),
        scratch_shapes=[
            pltpu.VMEM((row_blocks, width, tile), BF16),
            pltpu.VMEM((col_blocks + 1, width, tile), F32),
        ],
        compiler_params=room(WORK),
        cost_estimate=cost(work, 2 * tiles.size),
        name="backward_tiles",
    )(*ids, held, scale, *hids, *cots)
    backs = [backs[0]] + [swap(backs[k], "row", k) for k in range(1, n_rows)]
    input_grad = pl.pallas_call(
        grad_kernel,
        out_shape=jax.ShapeDtypeStruct((1, own, width), BF16),
        in_specs=[VMEM] * (2 + n_rows),
        out_specs=VMEM,
        compiler_params=room(8),
        name="input_grad",
    )(weight, relu_mask, *backs)

    for axis, size in (("col", n_cols), ("row", n_rows)):
        for bit in range(size.bit_length() - 1):
            weight_term = weight_term + swap(weight_term, axis, 1 << bit)
    return (out_pre, weight_term, input_grad)


def solution(mesh):
    placed = (
        P("col", "row", None),
        P("col", "row", None),
        P("row", "col", None, None, None),
        P("row", "col", None),
        P("row", "col", None),
        P("row", "col"),
        P(),
        P("row", "col", None),
    )
    return jax.shard_map(
        body,
        mesh=mesh,
        in_specs=placed,
        out_specs=(P("row", "col", None), P(), P("col", "row", None)),
        check_vma=False,
    )
```

```python
import functools
import math

import jax
import jax.numpy as jnp
from jax import lax
from jax.experimental import pallas as pl
from jax.experimental.pallas import tpu as pltpu
from jax.sharding import PartitionSpec as P

CORES = 2
MIB = 2**20
UNROLL = 23
WORK = 20
F32 = jnp.float32
BF16 = jnp.bfloat16
ANY = pl.BlockSpec(memory_space=pl.ANY)
SMEM = pl.BlockSpec(memory_space=pltpu.SMEM)
VMEM = pl.BlockSpec(memory_space=pltpu.VMEM)


def swap(value, axis, step):
    size = lax.axis_size(axis)
    return lax.ppermute(value, axis, [(i, i ^ step) for i in range(size)])


def room(size):
    return pltpu.CompilerParams(vmem_limit_bytes=size * MIB)


def cost(flops, moved):
    return pl.CostEstimate(flops=flops, bytes_accessed=moved, transcendentals=0)


def spot(k, count):
    return 0 if count == 1 else (k % 2) * (count // 2) + spot(k // 2, count // 2)


def load_kernel(count_ref, tiles, held, sems):
    chunk = held.shape[0] // sems.shape[0]
    chunks = pl.cdiv(count_ref[0, 0], chunk)

    def copy(i):
        span = pl.ds(i * chunk, chunk)
        return pltpu.make_async_copy(tiles.at[0, 0, span], held.at[span], sems.at[i])

    @pl.loop(0, chunks)
    def _(i):
        copy(i).start()

    @pl.loop(0, chunks)
    def _(i):
        copy(i).wait()


def for_slots(live, slots, work):
    unroll = math.gcd(slots, UNROLL)

    @pl.loop(0, pl.cdiv(live, unroll))
    def _(i):
        for j in range(unroll):
            work(i * unroll + j)


def forward_kernel(n_shards, count_ref, rows_ref, cols_ref, tiles, *refs):
    shards, (*outs, panel, acc) = refs[:n_shards], refs[n_shards:]
    slots, tile = tiles.shape[:2]
    own = shards[0].shape[0]
    dump = acc.shape[0] - 1
    live = count_ref[0, 0]
    row, col = lax.axis_index("row"), lax.axis_index("col")
    line, core = col // CORES, col % CORES

    acc[...] = jnp.zeros_like(acc)
    for k in range(n_shards):
        panel[pl.ds(pl.multiple_of((row ^ k) * own, own), own), :] = shards[k][...]

    def work(s):
        c = cols_ref[0, 0, s]
        r = jnp.where(s < live, rows_ref[0, 0, s], dump)
        source = panel[pl.ds(pl.multiple_of(c * tile, tile), tile), :]
        acc[r] += jnp.dot(tiles[s], source, preferred_element_type=F32)

    for_slots(live, slots, work)
    per = own // tile
    half = outs[0].shape[0] // own
    for k in range(2 * half):
        base = (line ^ k) * CORES
        part, place = divmod(spot(k, 2 * half), half)
        for b in range(per):
            span = pl.ds(place * own + b * tile, tile)
            outs[part][span, :] = acc[(base + core) * per + b].astype(BF16)
            span = pl.ds(b * tile, tile)
            outs[2 + spot(k, 2 * half)][span, :] = acc[(base + 1 - core) * per + b].astype(BF16)


def backward_kernel(n_rows, n_lines, count_ref, rows_ref, cols_ref, tiles, *refs):
    n_cots = n_lines * CORES
    cots, outs, (turned, acc) = refs[:n_cots], refs[n_cots:-2], refs[-2:]
    slots, tile = tiles.shape[:2]
    own = cots[0].shape[0]
    per = own // tile
    dump = acc.shape[0] - 1
    live = count_ref[0, 0]
    row, col = lax.axis_index("row"), lax.axis_index("col")
    line, core = col // CORES, col % CORES

    acc[...] = jnp.zeros_like(acc)
    for k in range(n_cots):
        place = ((line ^ (k // CORES)) * CORES + (core ^ (k % CORES))) * per
        for b in range(per):
            turned[place + b] = cots[k][b * tile : (b + 1) * tile, :].T

    def work(s):
        r = rows_ref[0, 0, s]
        c = jnp.where(s < live, cols_ref[0, 0, s], dump)
        acc[c] += jnp.dot(turned[r], tiles[s], preferred_element_type=F32)

    for_slots(live, slots, work)
    for k in range(n_rows):
        for b in range(per):
            outs[k][b * tile : (b + 1) * tile, :] = acc[(row ^ k) * per + b].T.astype(BF16)


def weight_kernel(scale, stay, away, *refs):
    *cots, out = refs
    own = cots[0].shape[0]
    total = jnp.zeros(out.shape, F32)
    for k, cot in enumerate(cots):
        side, place = divmod(spot(k, len(cots)), len(cots) // 2)
        part = (stay, away)[side][place * own : (place + 1) * own, :]
        total += lax.dot_general(
            part, cot[...], (((0,), (0,)), ((), ())), preferred_element_type=F32
        )
    out[...] = total * scale[0]


def merge_kernel(keep, *refs):
    *got, out = refs
    for k, part in enumerate(got):
        span = pl.ds(k * part.shape[0], part.shape[0])
        out[span, :] = (keep[span, :].astype(F32) + part[...].astype(F32)).astype(BF16)


def add_kernel(start, left, right, out):
    span = pl.ds(start, out.shape[0])
    out[...] = (left[span, :].astype(F32) + right[span, :].astype(F32)).astype(BF16)


def summed(parts):
    total = parts[0][...].astype(F32)
    for part in parts[1:]:
        total += part[...].astype(F32)
    return total.astype(BF16)


def finish_kernel(n_rows, weight, mask, stay, got, *refs):
    backs, terms = refs[:n_rows], refs[n_rows:-3]
    out_pre, weight_grad, input_grad = refs[-3:]
    weights = weight[...]
    out_pre[0] = jnp.dot(summed((stay, got)), weights, preferred_element_type=F32).astype(BF16)
    weight_grad[...] = tree([term[...] for term in terms])
    grads = lax.dot_general(
        summed(backs), weights, (((1,), (1,)), ((), ())), preferred_element_type=F32
    )
    input_grad[0] = (grads * mask[0].astype(F32)).astype(BF16)


def tree(terms):
    while len(terms) > 1:
        terms = [a + b for a, b in zip(terms[::2], terms[1::2])]
    return terms[0]


def body(features, relu_mask, tiles, tile_rows, tile_cols, tile_count, weight, cotangent):
    slots, tile = tiles.shape[2:4]
    own, width = features.shape[1:]
    n_rows, n_cols = lax.axis_size("row"), lax.axis_size("col")
    n_lines = n_cols // CORES
    row_blocks, col_blocks = own * n_cols // tile, own * n_rows // tile
    ids = (tile_count, tile_rows, tile_cols)
    block = jax.ShapeDtypeStruct((own, width), BF16)
    work = 2 * tiles.size * width

    cot = cotangent[0]
    cots = [cot] + [swap(cot, "col", CORES * k) for k in range(1, n_lines)]
    cots = [part for mine in cots for part in (mine, swap(mine, "col", 1))]
    hidden = features[0] * relu_mask[0].astype(BF16)
    hids = [hidden] + [swap(hidden, "row", k) for k in range(1, n_rows)]

    held = pl.pallas_call(
        load_kernel,
        out_shape=jax.ShapeDtypeStruct((slots, tile, tile), BF16),
        in_specs=[SMEM, ANY],
        out_specs=VMEM,
        scratch_shapes=[pltpu.SemaphoreType.DMA((slots // math.gcd(slots, 8),))],
        compiler_params=room(WORK),
        cost_estimate=cost(0, 2 * tiles.size),
        name="load_tiles",
    )(tile_count, tiles)

    half = jax.ShapeDtypeStruct((n_lines * own // 2, width), BF16)
    keep_stay, keep_away, *send = pl.pallas_call(
        functools.partial(forward_kernel, n_rows),
        out_shape=(half,) * 2 + (block,) * n_lines,
        in_specs=[SMEM] * 3 + [VMEM] * (1 + n_rows),
        out_specs=(VMEM,) * (2 + n_lines),
        scratch_shapes=[
            pltpu.VMEM((n_rows * own, width), BF16),
            pltpu.VMEM((row_blocks + 1, tile, width), F32),
        ],
        compiler_params=room(WORK),
        cost_estimate=cost(work, 2 * tiles.size),
        name="forward_tiles",
    )(*ids, held, *hids)

    def merge(keep, got):
        return pl.pallas_call(
            merge_kernel,
            out_shape=half,
            in_specs=[VMEM] * (1 + len(got)),
            out_specs=VMEM,
            compiler_params=room(8),
            name="merge_parts",
        )(keep, *got)

    def add(left, right, start, count):
        return pl.pallas_call(
            functools.partial(add_kernel, start * own),
            out_shape=jax.ShapeDtypeStruct((count * own, width), BF16),
            in_specs=[VMEM] * 2,
            out_specs=VMEM,
            compiler_params=room(8),
            name="add_parts",
        )(left, right)

    pairs = [swap(part, "col", 1) for part in send]
    got_stay, got_away = pairs[: n_lines // 2], pairs[n_lines // 2 :]
    away = merge(keep_away, got_away)
    got_stay, cots = lax.optimization_barrier((got_stay, cots))
    stay = merge(keep_stay, got_stay)
    got = swap(away, "col", CORES)
    scale = 1.0 / jnp.sqrt(jnp.full((1,), own * n_rows * n_cols, F32))
    weight_term = pl.pallas_call(
        weight_kernel,
        out_shape=jax.ShapeDtypeStruct((width, width), F32),
        in_specs=[SMEM] + [VMEM] * (2 + n_lines),
        out_specs=VMEM,
        compiler_params=room(8),
        name="weight_term",
    )(scale, stay, away, *cots[::CORES])

    backs = pl.pallas_call(
        functools.partial(backward_kernel, n_rows, n_lines),
        out_shape=(block,) * n_rows,
        in_specs=[SMEM] * 3 + [VMEM] * (1 + n_cols),
        out_specs=(VMEM,) * n_rows,
        scratch_shapes=[
            pltpu.VMEM((row_blocks, width, tile), BF16),
            pltpu.VMEM((col_blocks + 1, width, tile), F32),
        ],
        compiler_params=room(WORK),
        cost_estimate=cost(work, 2 * tiles.size),
        name="backward_tiles",
    )(*ids, held, *cots)
    weight_term = weight_term + swap(weight_term, "col", 1)
    terms = [weight_term] + [swap(weight_term, "row", k) for k in range(1, n_rows)]
    backs, terms, got = lax.optimization_barrier((backs, terms, got))
    weight_term = tree(terms)
    bit, count = 1, n_lines // 2
    while count > 1:
        count, bit = count // 2, 2 * bit
        away = swap(add(stay, got, count, count), "col", CORES * bit)
        stay, got = add(stay, got, 0, count), away
    backs = [backs[0]] + [swap(backs[k], "row", k) for k in range(1, n_rows)]
    for b in range(n_lines.bit_length() - 2):
        weight_term = weight_term + swap(weight_term, "col", CORES << b)
    terms = [weight_term, swap(weight_term, "col", n_cols // 2)]
    block = jax.ShapeDtypeStruct((1, own, width), BF16)
    return pl.pallas_call(
        functools.partial(finish_kernel, n_rows),
        out_shape=(block, jax.ShapeDtypeStruct((width, width), F32), block),
        in_specs=[VMEM] * (4 + n_rows + len(terms)),
        out_specs=(VMEM,) * 3,
        compiler_params=room(8),
        name="finish",
    )(weight, relu_mask, stay, got, *backs, *terms)


def solution(mesh):
    placed = (
        P("col", "row", None),
        P("col", "row", None),
        P("row", "col", None, None, None),
        P("row", "col", None),
        P("row", "col", None),
        P("row", "col"),
        P(),
        P("row", "col", None),
    )
    return jax.shard_map(
        body,
        mesh=mesh,
        in_specs=placed,
        out_specs=(P("row", "col", None), P(), P("col", "row", None)),
        check_vma=False,
    )
```

```python
import functools
import math

import jax
import jax.numpy as jnp
from jax import lax
from jax.experimental import pallas as pl
from jax.experimental.pallas import tpu as pltpu
from jax.sharding import PartitionSpec as P

CORES = 2
MIB = 2**20
UNROLL = 92
WORK = 20
F32 = jnp.float32
BF16 = jnp.bfloat16
ANY = pl.BlockSpec(memory_space=pl.ANY)
SMEM = pl.BlockSpec(memory_space=pltpu.SMEM)
VMEM = pl.BlockSpec(memory_space=pltpu.VMEM)


def swap(value, axis, step):
    size = lax.axis_size(axis)
    return lax.ppermute(value, axis, [(i, i ^ step) for i in range(size)])


def room(size):
    return pltpu.CompilerParams(vmem_limit_bytes=size * MIB)


def cost(flops, moved):
    return pl.CostEstimate(flops=flops, bytes_accessed=moved, transcendentals=0)


def spot(k, count):
    return 0 if count == 1 else (k % 2) * (count // 2) + spot(k // 2, count // 2)


def tile_copies(tiles, start, count, live):
    chunk = math.gcd(count, 4)

    def copy(held, sems, i):
        source = tiles.at[0, 0, pl.ds(start + i * chunk, chunk)]
        return pltpu.make_async_copy(source, held.at[pl.ds(i * chunk, chunk)], sems.at[i])

    needed = jnp.minimum(pl.cdiv(jnp.maximum(live - start, 0), chunk), count // chunk)
    return copy, needed


def load_kernel(count_ref, tiles, held, sems):
    copy, needed = tile_copies(tiles, 0, held.shape[0], count_ref[0, 0])

    @pl.loop(0, needed)
    def _(i):
        copy(held, sems, i).start()

    @pl.loop(0, needed)
    def _(i):
        copy(held, sems, i).wait()


def for_slots(live, held, start, work):
    count = held.shape[0]
    unroll = math.gcd(count, UNROLL)
    passes = jnp.minimum(pl.cdiv(jnp.maximum(live - start, 0), unroll), count // unroll)

    @pl.loop(0, passes)
    def _(i):
        for j in range(unroll):
            at = i * unroll + j
            work(start + at, held, at)


def forward_kernel(n_shards, count_ref, rows_ref, cols_ref, held, tiles, *refs):
    shards, (rest, *outs, panel, acc, sems) = refs[:n_shards], refs[n_shards:]
    start, tile = held.shape[:2]
    own = shards[0].shape[0]
    dump = acc.shape[0] - 1
    live = count_ref[0, 0]
    row, col = lax.axis_index("row"), lax.axis_index("col")
    line, core = col // CORES, col % CORES

    copy, needed = tile_copies(tiles, start, rest.shape[0], live)

    @pl.loop(0, needed)
    def _(i):
        copy(rest, sems, i).start()

    acc[...] = jnp.zeros_like(acc)
    for k in range(n_shards):
        panel[pl.ds(pl.multiple_of((row ^ k) * own, own), own), :] = shards[k][...]

    def work(s, block, at):
        c = cols_ref[0, 0, s]
        r = jnp.where(s < live, rows_ref[0, 0, s], dump)
        source = panel[pl.ds(pl.multiple_of(c * tile, tile), tile), :]
        acc[r] += jnp.dot(block[at], source, preferred_element_type=F32)

    for_slots(live, held, 0, work)

    @pl.loop(0, needed)
    def _(i):
        copy(rest, sems, i).wait()

    for_slots(live, rest, start, work)
    per = own // tile
    half = outs[0].shape[0] // own
    for k in range(2 * half):
        base = (line ^ k) * CORES
        part, place = divmod(spot(k, 2 * half), half)
        for b in range(per):
            span = pl.ds(place * own + b * tile, tile)
            outs[part][span, :] = acc[(base + core) * per + b].astype(BF16)
            span = pl.ds(b * tile, tile)
            outs[2 + spot(k, 2 * half)][span, :] = acc[(base + 1 - core) * per + b].astype(BF16)


def backward_kernel(n_rows, n_lines, count_ref, rows_ref, cols_ref, held, rest, *refs):
    n_cots = n_lines * CORES
    cots, outs, (turned, acc) = refs[:n_cots], refs[n_cots:-2], refs[-2:]
    start, tile = held.shape[:2]
    own = cots[0].shape[0]
    per = own // tile
    dump = acc.shape[0] - 1
    live = count_ref[0, 0]
    row, col = lax.axis_index("row"), lax.axis_index("col")
    line, core = col // CORES, col % CORES

    acc[...] = jnp.zeros_like(acc)
    for k in range(n_cots):
        place = ((line ^ (k // CORES)) * CORES + (core ^ (k % CORES))) * per
        for b in range(per):
            turned[place + b] = cots[k][b * tile : (b + 1) * tile, :].T

    def work(s, block, at):
        r = rows_ref[0, 0, s]
        c = jnp.where(s < live, cols_ref[0, 0, s], dump)
        acc[c] += jnp.dot(turned[r], block[at], preferred_element_type=F32)

    for_slots(live, held, 0, work)
    for_slots(live, rest, start, work)
    for k in range(n_rows):
        for b in range(per):
            outs[k][b * tile : (b + 1) * tile, :] = acc[(row ^ k) * per + b].astype(BF16).T


def weight_kernel(scale, stay, away, *refs):
    *cots, out = refs
    own = cots[0].shape[0]
    total = jnp.zeros(out.shape, F32)
    for k, cot in enumerate(cots):
        side, place = divmod(spot(k, len(cots)), len(cots) // 2)
        part = (stay, away)[side][place * own : (place + 1) * own, :]
        total += lax.dot_general(
            part, cot[...], (((0,), (0,)), ((), ())), preferred_element_type=F32
        )
    out[...] = total * scale[0]


def merge_kernel(keep, *refs):
    *got, out = refs
    for k, part in enumerate(got):
        span = pl.ds(k * part.shape[0], part.shape[0])
        out[span, :] = (keep[span, :].astype(F32) + part[...].astype(F32)).astype(BF16)


def add_kernel(start, left, right, out):
    span = pl.ds(start, out.shape[0])
    out[...] = (left[span, :].astype(F32) + right[span, :].astype(F32)).astype(BF16)


def summed(parts):
    total = parts[0][...].astype(F32)
    for part in parts[1:]:
        total += part[...].astype(F32)
    return total.astype(BF16)


def finish_kernel(n_rows, weight, mask, stay, got, *refs):
    backs, terms = refs[:n_rows], refs[n_rows:-3]
    out_pre, weight_grad, input_grad = refs[-3:]
    weights = weight[...]
    out_pre[0] = jnp.dot(summed((stay, got)), weights, preferred_element_type=F32).astype(BF16)
    weight_grad[...] = tree([term[...] for term in terms])
    grads = lax.dot_general(
        summed(backs), weights, (((1,), (1,)), ((), ())), preferred_element_type=F32
    )
    input_grad[0] = (grads * mask[0].astype(F32)).astype(BF16)


def tree(terms):
    while len(terms) > 1:
        terms = [a + b for a, b in zip(terms[::2], terms[1::2])]
    return terms[0]


def body(features, relu_mask, tiles, tile_rows, tile_cols, tile_count, weight, cotangent):
    slots, tile = tiles.shape[2:4]
    own, width = features.shape[1:]
    n_rows, n_cols = lax.axis_size("row"), lax.axis_size("col")
    n_lines = n_cols // CORES
    row_blocks, col_blocks = own * n_cols // tile, own * n_rows // tile
    ids = (tile_count, tile_rows, tile_cols)
    block = jax.ShapeDtypeStruct((own, width), BF16)
    work = 2 * tiles.size * width

    cot = cotangent[0]
    cots = [cot] + [swap(cot, "col", CORES * k) for k in range(1, n_lines)]
    cots = [part for mine in cots for part in (mine, swap(mine, "col", 1))]
    hidden = features[0] * relu_mask[0].astype(BF16)
    hids = [hidden] + [swap(hidden, "row", k) for k in range(1, n_rows)]

    part = jax.ShapeDtypeStruct((slots // 2, tile, tile), BF16)
    held = pl.pallas_call(
        load_kernel,
        out_shape=part,
        in_specs=[SMEM, ANY],
        out_specs=VMEM,
        scratch_shapes=[pltpu.SemaphoreType.DMA((slots // 2 // math.gcd(slots // 2, 4),))],
        compiler_params=room(WORK),
        cost_estimate=cost(0, 2 * tiles.size),
        name="load_tiles",
    )(tile_count, tiles)

    half = jax.ShapeDtypeStruct((n_lines * own // 2, width), BF16)
    rest, keep_stay, keep_away, *send = pl.pallas_call(
        functools.partial(forward_kernel, n_rows),
        out_shape=(part,) + (half,) * 2 + (block,) * n_lines,
        in_specs=[SMEM] * 3 + [VMEM, ANY] + [VMEM] * n_rows,
        out_specs=(VMEM,) * (3 + n_lines),
        scratch_shapes=[
            pltpu.VMEM((n_rows * own, width), BF16),
            pltpu.VMEM((row_blocks + 1, tile, width), F32),
            pltpu.SemaphoreType.DMA((slots // 2 // math.gcd(slots // 2, 4),)),
        ],
        compiler_params=room(WORK),
        cost_estimate=cost(work, 2 * tiles.size),
        name="forward_tiles",
    )(*ids, held, tiles, *hids)

    def merge(keep, got):
        return pl.pallas_call(
            merge_kernel,
            out_shape=half,
            in_specs=[VMEM] * (1 + len(got)),
            out_specs=VMEM,
            compiler_params=room(8),
            name="merge_parts",
        )(keep, *got)

    def add(left, right, start, count):
        return pl.pallas_call(
            functools.partial(add_kernel, start * own),
            out_shape=jax.ShapeDtypeStruct((count * own, width), BF16),
            in_specs=[VMEM] * 2,
            out_specs=VMEM,
            compiler_params=room(8),
            name="add_parts",
        )(left, right)

    pairs = [swap(part, "col", 1) for part in send]
    got_stay, got_away = pairs[: n_lines // 2], pairs[n_lines // 2 :]
    away = merge(keep_away, got_away)
    got_stay, cots = lax.optimization_barrier((got_stay, cots))
    stay = merge(keep_stay, got_stay)
    got = swap(away, "col", CORES)
    scale = 1.0 / jnp.sqrt(jnp.full((1,), own * n_rows * n_cols, F32))
    weight_term = pl.pallas_call(
        weight_kernel,
        out_shape=jax.ShapeDtypeStruct((width, width), F32),
        in_specs=[SMEM] + [VMEM] * (2 + n_lines),
        out_specs=VMEM,
        compiler_params=room(8),
        name="weight_term",
    )(scale, stay, away, *cots[::CORES])

    backs = pl.pallas_call(
        functools.partial(backward_kernel, n_rows, n_lines),
        out_shape=(block,) * n_rows,
        in_specs=[SMEM] * 3 + [VMEM] * (2 + n_cols),
        out_specs=(VMEM,) * n_rows,
        scratch_shapes=[
            pltpu.VMEM((row_blocks, width, tile), BF16),
            pltpu.VMEM((col_blocks + 1, width, tile), F32),
        ],
        compiler_params=room(WORK),
        cost_estimate=cost(work, 2 * tiles.size),
        name="backward_tiles",
    )(*ids, held, rest, *cots)
    weight_term = weight_term + swap(weight_term, "col", 1)
    terms = [weight_term] + [swap(weight_term, "row", k) for k in range(1, n_rows)]
    backs, terms, got = lax.optimization_barrier((backs, terms, got))
    weight_term = tree(terms)
    bit, count = 1, n_lines // 2
    while count > 1:
        count, bit = count // 2, 2 * bit
        away = swap(add(stay, got, count, count), "col", CORES * bit)
        stay, got = add(stay, got, 0, count), away
    backs = [backs[0]] + [swap(backs[k], "row", k) for k in range(1, n_rows)]
    for b in range(n_lines.bit_length() - 2):
        weight_term = weight_term + swap(weight_term, "col", CORES << b)
    terms = [weight_term, swap(weight_term, "col", n_cols // 2)]
    block = jax.ShapeDtypeStruct((1, own, width), BF16)
    return pl.pallas_call(
        functools.partial(finish_kernel, n_rows),
        out_shape=(block, jax.ShapeDtypeStruct((width, width), F32), block),
        in_specs=[VMEM] * (4 + n_rows + len(terms)),
        out_specs=(VMEM,) * 3,
        compiler_params=room(8),
        name="finish",
    )(weight, relu_mask, stay, got, *backs, *terms)


def solution(mesh):
    placed = (
        P("col", "row", None),
        P("col", "row", None),
        P("row", "col", None, None, None),
        P("row", "col", None),
        P("row", "col", None),
        P("row", "col"),
        P(),
        P("row", "col", None),
    )
    return jax.shard_map(
        body,
        mesh=mesh,
        in_specs=placed,
        out_specs=(P("row", "col", None), P(), P("col", "row", None)),
        check_vma=False,
    )
```
